32 devices in a mesh: frame: 8 (over y, x, core), head: 4 (over z).
Axes of the slice: x: 2, y: 2, z: 4, core: 2. Of those that a mesh axis runs over, the one named last changes fastest.
Arguments:
- queries: bfloat16 [8192, 5120], P(('frame', 'head'))
- keys: bfloat16 [8192, 5120], P(('frame', 'head'))
- values: bfloat16 [8192, 5120], P(('frame', 'head')), may hold values from -6 to 6
- out_grad: bfloat16 [8192, 5120], P(('frame', 'head')), may hold values from -6 to 6
- memory_frames: int32 [8, 7], replicated, may hold values from 0 to 127, as said below
- frame_tokens: int32 [128], replicated, may hold values from 32 to 64
Outputs:
- attn_out: bfloat16 [8192, 5120], P(('frame', 'head'))
- query_grad: bfloat16 [8192, 5120], P(('frame', 'head'))
- key_grad: bfloat16 [8192, 5120], P(('frame', 'head'))
- value_grad: bfloat16 [8192, 5120], P(('frame', 'head'))
The draws below stay inside these ranges and needn't reach their ends.
Inputs may be any that keep to these rules, and one draw needn't show every extreme that they name: `memory_frames`: entry i of row c names a frame of group (c - 1 - i) mod 8.
All inputs are finite; a program needn't handle non-finite values.
Results may differ from the reference program's by a relative error of at most 0.0069.
Values may be sent and summed in bfloat16 or wider, within the bound.
A program may use at most 320 MiB of HBM per device.

```python
import math
import jax
import jax.numpy as jnp
from jax import lax

HEADS = 40
HEAD_DIM = 128
TF = 64
FRAMES_DEV = 16
GROUPS = 8
OWNERS = 7
FEAT = 5120
FRAMES = 128
TOKENS = 8192


def draw_queries(key, part):
    key = jax.random.fold_in(key, 11)
    field = jnp.clip(jax.random.normal(key, (FRAMES, TF, FEAT), jnp.float32), -6.0, 6.0)
    return field.reshape(TOKENS, FEAT).astype(jnp.bfloat16)


def draw_keys(key, part):
    key = jax.random.fold_in(key, 12)
    field = jnp.clip(jax.random.normal(key, (FRAMES, TF, FEAT), jnp.float32), -6.0, 6.0)
    return field.reshape(TOKENS, FEAT).astype(jnp.bfloat16)


def draw_frame_tokens(key, part):
    key = jax.random.fold_in(key, 21)
    counts = jax.random.randint(key, (FRAMES,), TF // 2, TF + 1, dtype=jnp.int32)
    index = jnp.arange(FRAMES, dtype=jnp.int32)
    return jnp.where(index == 0, TF, jnp.where(index == 1, TF // 2, counts)).astype(jnp.int32)


def draw_memory_frames(key, part):
    key = jax.random.fold_in(key, 31)
    group_ids = jnp.arange(GROUPS, dtype=jnp.int32)
    slot_ids = jnp.arange(OWNERS, dtype=jnp.int32)
    owner_group = (group_ids[:, None] - 1 - slot_ids[None, :]) % GROUPS
    within = jax.random.randint(key, (GROUPS, OWNERS), 0, FRAMES_DEV, dtype=jnp.int32)
    return (owner_group * FRAMES_DEV + within).astype(jnp.int32)


def level_of(rng, dims, shards, least, largest):
    def one(position, shards_of):
        heights = jax.random.uniform(jax.random.fold_in(jax.random.fold_in(rng, 6), position), (shards_of,), jnp.float32, least / len(shards), largest / len(shards))
        return jnp.repeat(jnp.exp(heights), dims[position] // shards_of).reshape((-1,) + (1,) * (len(dims) - position - 1))

    level = one(*shards[0])
    for cut in shards[1:]:
        level = level * one(*cut)
    return level


def scatter_about(stream_key, extent, scale, most, cuts=(), kind=jnp.bfloat16):
    level = level_of(stream_key, extent, cuts, -0.22, 0.18) if cuts else 1.0
    result = jax.random.normal(stream_key, extent, jnp.float32) * scale * level
    return jnp.minimum(jnp.maximum(result, -most), most).astype(kind)


def setup_inputs(seed: int = 0) -> dict:
    key_of = jax.random.split(jax.random.key(seed), 7)
    return {
        "queries": draw_queries(jax.random.fold_in(key_of[6], 71), 0),
        "keys": draw_keys(jax.random.fold_in(key_of[6], 71), 0),
        "values": scatter_about(key_of[2], (TOKENS, FEAT), 1.0, 6.0, ((0, 32),)),
        "out_grad": scatter_about(key_of[3], (TOKENS, FEAT), 1.0, 6.0, ((0, 32),)),
        "memory_frames": draw_memory_frames(jax.random.fold_in(key_of[6], 71), 0),
        "frame_tokens": draw_frame_tokens(jax.random.fold_in(key_of[6], 71), 0),
    }


def reference(queries, keys, values, out_grad, memory_frames, frame_tokens):
    group_rows = FRAMES_DEV * TF
    score_scale = 1.0 / math.sqrt(HEAD_DIM)
    token_pos = jnp.arange(TF, dtype=jnp.int32)
    live_mask = token_pos[None, :] < frame_tokens[:, None]
    live_groups = live_mask.reshape(GROUPS, group_rows)
    query_groups = queries.reshape(GROUPS, group_rows, HEADS, HEAD_DIM)
    key_groups = keys.reshape(GROUPS, group_rows, HEADS, HEAD_DIM)
    value_groups = values.reshape(GROUPS, group_rows, HEADS, HEAD_DIM)
    grad_groups = out_grad.reshape(GROUPS, group_rows, HEADS, HEAD_DIM)
    key_frames = keys.reshape(FRAMES, TF, HEADS, HEAD_DIM)
    value_frames = values.reshape(FRAMES, TF, HEADS, HEAD_DIM)

    def one_group(group_id):
        chosen = memory_frames[group_id]
        key_set = jnp.concatenate([key_groups[group_id], key_frames[chosen].reshape(OWNERS * TF, HEADS, HEAD_DIM)], 0)
        value_set = jnp.concatenate([value_groups[group_id], value_frames[chosen].reshape(OWNERS * TF, HEADS, HEAD_DIM)], 0)
        live_set = jnp.concatenate([live_groups[group_id], live_mask[chosen].reshape(OWNERS * TF)], 0)
        query_wide = query_groups[group_id].astype(jnp.float32)
        grad_wide = grad_groups[group_id].astype(jnp.float32)
        key_wide = key_set.astype(jnp.float32)
        value_wide = value_set.astype(jnp.float32)
        scores = jnp.einsum('rhd,khd->hrk', query_wide, key_wide) * score_scale
        scores = jnp.where(live_set[None, None, :], scores, -jnp.inf)
        row_top = lax.optimization_barrier(jnp.max(scores, axis=2, keepdims=True))
        powers = jnp.exp(scores - row_top)
        weights = powers / lax.optimization_barrier(jnp.sum(powers, axis=2, keepdims=True))
        weights_b = weights.astype(jnp.bfloat16).astype(jnp.float32)
        attn_out = jnp.einsum('hrk,khd->rhd', weights_b, value_wide).astype(jnp.bfloat16)
        weight_grads = jnp.einsum('rhd,khd->hrk', grad_wide, value_wide)
        row_delta = lax.optimization_barrier(jnp.sum(weights * weight_grads, axis=2, keepdims=True))
        score_grads = (weights * (weight_grads - row_delta)).astype(jnp.bfloat16).astype(jnp.float32)
        query_grad = (jnp.einsum('hrk,khd->rhd', score_grads, key_wide) * score_scale).astype(jnp.bfloat16)
        key_part = jnp.einsum('hrk,rhd->khd', score_grads, query_wide) * score_scale
        value_part = jnp.einsum('hrk,rhd->khd', weights_b, grad_wide)
        return (attn_out, query_grad, key_part[:group_rows], value_part[:group_rows], key_part[group_rows:].astype(jnp.bfloat16), value_part[group_rows:].astype(jnp.bfloat16))
    attn_out, query_grad, own_kg, own_vg, mem_kg, mem_vg = lax.map(one_group, jnp.arange(GROUPS, dtype=jnp.int32))
    frame_ids = memory_frames.reshape(GROUPS * OWNERS)
    key_extra = jax.ops.segment_sum(mem_kg.reshape(GROUPS * OWNERS, TF * FEAT).astype(jnp.float32), frame_ids, num_segments=FRAMES)
    value_extra = jax.ops.segment_sum(mem_vg.reshape(GROUPS * OWNERS, TF * FEAT).astype(jnp.float32), frame_ids, num_segments=FRAMES)
    key_grad = (own_kg.reshape(FRAMES, TF * FEAT) + key_extra).astype(jnp.bfloat16).reshape(TOKENS, FEAT)
    value_grad = (own_vg.reshape(FRAMES, TF * FEAT) + value_extra).astype(jnp.bfloat16).reshape(TOKENS, FEAT)
    return (attn_out.reshape(TOKENS, FEAT), query_grad.reshape(TOKENS, FEAT), key_grad, value_grad)
```

```python
import functools
import math

import jax
import jax.numpy as jnp
from jax import lax
from jax.experimental import pallas as pl
from jax.experimental.pallas import tpu as pltpu
from jax.sharding import PartitionSpec as P

HEAD_DIM = 128
TF = 64
FRAMES_DEV = 16
ROWS = FRAMES_DEV * TF
QBLOCK = 256
AHEAD = 4
MESH = pl.DeviceIdType.MESH


def attention_kernel(
    dims,
    q_in, k_in, v_in, g_in, bias_ref, pick_ref, spread_ref,
    o_out, dq_out, dk_out, dv_out,
    qg, kv, mem_send, mem_grad, back, outs, acc,
    in_send, in_recv, mem_ssem, mem_rsem, back_ssem, back_rsem, out_send, out_recv,
):
    groups, zs, heads, slots, part, key_rows = dims
    mem_rows = slots * TF
    scale = 1.0 / math.sqrt(HEAD_DIM)
    g = lax.axis_index("frame")
    z = lax.axis_index("head")

    barrier = pltpu.get_barrier_semaphore()
    offsets = sorted({(1 + i) % groups for i in range(slots)} | {(-1 - i) % groups for i in range(slots)})
    for off in offsets:
        pl.semaphore_signal(
            barrier, inc=1, device_id={"frame": lax.rem(g + off, groups)}, device_id_type=MESH
        )
    for off in range(1, zs):
        pl.semaphore_signal(
            barrier, inc=1, device_id={"head": lax.rem(z + off, zs)}, device_id_type=MESH
        )
    pl.semaphore_wait(barrier, len(offsets) + zs - 1)

    my_rows = pl.ds(pl.multiple_of(z * part, part), part)

    def landing(h, a, rows):
        if a < 2:
            return kv.at[h, a, rows]
        return qg.at[h, a - 2, rows]

    def send_inputs(h):
        for a, src in enumerate((k_in, v_in, q_in, g_in)):
            for off in range(zs - 1, 0, -1):
                peer = lax.rem(z + off, zs)
                cols = pl.ds(pl.multiple_of((peer * heads + h) * HEAD_DIM, HEAD_DIM), HEAD_DIM)
                pltpu.make_async_remote_copy(
                    src_ref=src.at[:, cols],
                    dst_ref=landing(h, a, my_rows),
                    send_sem=in_send.at[a],
                    recv_sem=in_recv.at[h, a],
                    device_id={"head": peer},
                    device_id_type=MESH,
                ).start()
            cols = pl.ds(pl.multiple_of((z * heads + h) * HEAD_DIM, HEAD_DIM), HEAD_DIM)
            pltpu.make_async_copy(
                src.at[:, cols], landing(h, a, my_rows), in_recv.at[h, a]
            ).start()

    def wait_for(ref, sem):
        pltpu.make_async_copy(ref, ref, sem).wait()

    def send_output(h, a):
        dst = (o_out, dq_out, dk_out, dv_out)[a]
        cols = pl.ds(pl.multiple_of((z * heads + h) * HEAD_DIM, HEAD_DIM), HEAD_DIM)
        for off in range(zs - 1, 0, -1):
            peer = lax.rem(z + off, zs)
            pltpu.make_async_remote_copy(
                src_ref=outs.at[h, a, pl.ds(pl.multiple_of(peer * part, part), part)],
                dst_ref=dst.at[:, cols],
                send_sem=out_send.at[a],
                recv_sem=out_recv.at[a],
                device_id={"head": peer},
                device_id_type=MESH,
            ).start()
        pltpu.make_async_copy(outs.at[h, a, my_rows], dst.at[:, cols], out_recv.at[a]).start()

    lax.fori_loop(0, min(AHEAD, heads), lambda h, c: (send_inputs(h), c)[1], 0)

    if key_rows > ROWS + mem_rows:
        rest = key_rows - ROWS - mem_rows

        def clear(h, c):
            kv[h, :, ROWS + mem_rows :, :] = jnp.zeros((2, rest, HEAD_DIM), jnp.bfloat16)
            return c

        lax.fori_loop(0, heads, clear, 0)

    def fetch(h):
        for a in range(2):
            wait_for(landing(h, a, pl.ds(0, ROWS)), in_recv.at[h, a])
        for a in range(2):
            mem_send[h, a] = jnp.dot(
                pick_ref[...], kv[h, a, :ROWS, :], preferred_element_type=jnp.float32
            ).astype(jnp.bfloat16)
        for i in range(slots):
            pltpu.make_async_remote_copy(
                src_ref=mem_send.at[h, :, pl.ds(i * TF, TF)],
                dst_ref=kv.at[h, :, pl.ds(ROWS + i * TF, TF)],
                send_sem=mem_ssem,
                recv_sem=mem_rsem.at[h],
                device_id={"frame": lax.rem(g + 1 + i, groups)},
                device_id_type=MESH,
            ).start()

    def attend(h):
        slot = lax.rem(h, 2)
        for a in range(2, 4):
            wait_for(landing(h, a, pl.ds(0, ROWS)), in_recv.at[h, a])
        wait_for(kv.at[h, :, pl.ds(ROWS, mem_rows)], mem_rsem.at[h])
        acc[slot] = jnp.zeros(acc.shape[1:], jnp.float32)

        def block(b, c):
            rows = pl.ds(pl.multiple_of(b * QBLOCK, QBLOCK), QBLOCK)
            query = qg[h, 0, rows, :]
            grad = qg[h, 1, rows, :]
            key = kv[h, 0]
            value = kv[h, 1]
            s = lax.dot_general(
                query, key, (((1,), (1,)), ((), ())), preferred_element_type=jnp.float32
            )
            s = s * (scale * math.log2(math.e)) + bias_ref[...]
            p = jnp.exp2(s - jnp.max(s, axis=1, keepdims=True))
            w = p * (1.0 / jnp.sum(p, axis=1, keepdims=True))
            wb = w.astype(jnp.bfloat16)
            outs[h, 0, rows, :] = jnp.dot(
                wb, value, preferred_element_type=jnp.float32
            ).astype(jnp.bfloat16)
            dp = lax.dot_general(
                grad, value, (((1,), (1,)), ((), ())), preferred_element_type=jnp.float32
            )
            delta = jnp.sum(w * dp, axis=1, keepdims=True)
            ds = (w * (dp - delta)).astype(jnp.bfloat16)
            outs[h, 1, rows, :] = (
                jnp.dot(ds, key, preferred_element_type=jnp.float32) * scale
            ).astype(jnp.bfloat16)
            acc[slot, 0] += lax.dot_general(
                ds, query, (((0,), (0,)), ((), ())), preferred_element_type=jnp.float32
            )
            acc[slot, 1] += lax.dot_general(
                wb, grad, (((0,), (0,)), ((), ())), preferred_element_type=jnp.float32
            )
            return c

        lax.fori_loop(0, ROWS // QBLOCK, block, 0)
        mem = pl.ds(ROWS, mem_rows)
        mem_grad[h, 0] = (acc[slot, 0, mem, :] * scale).astype(jnp.bfloat16)
        mem_grad[h, 1] = acc[slot, 1, mem, :].astype(jnp.bfloat16)
        for i in range(slots):
            pltpu.make_async_remote_copy(
                src_ref=mem_grad.at[h, :, pl.ds(i * TF, TF)],
                dst_ref=back.at[h, :, pl.ds(i * TF, TF)],
                send_sem=back_ssem,
                recv_sem=back_rsem.at[h],
                device_id={"frame": lax.rem(g + groups - 1 - i, groups)},
                device_id_type=MESH,
            ).start()
        send_output(h, 0)
        send_output(h, 1)

    def finish(h):
        slot = lax.rem(h, 2)
        wait_for(back.at[h], back_rsem.at[h])
        for a in range(2):
            extra = jnp.dot(spread_ref[...], back[h, a], preferred_element_type=jnp.float32)
            own = acc[slot, a, :ROWS, :]
            if a == 0:
                own = own * scale
            outs[h, 2 + a] = (own + extra).astype(jnp.bfloat16)
            send_output(h, 2 + a)

    def step(t, c):
        @pl.when(t < heads - AHEAD)
        def _():
            send_inputs(t + AHEAD)

        @pl.when(t < heads)
        def _():
            fetch(t)

        @pl.when(t >= 2)
        def _():
            finish(t - 2)

        @pl.when(jnp.logical_and(t >= 1, t <= heads))
        def _():
            attend(t - 1)

        return c

    lax.fori_loop(0, heads + 2, step, 0)

    sent = pl.ds(0, (zs - 1) * heads * HEAD_DIM)
    for a, src in enumerate((k_in, v_in, q_in, g_in)):
        wait_for(src.at[:, sent], in_send.at[a])
    wait_for(mem_send, mem_ssem)
    wait_for(mem_grad, back_ssem)
    for a, dst in enumerate((o_out, dq_out, dk_out, dv_out)):
        wait_for(outs.at[:, a, pl.ds(0, (zs - 1) * part)], out_send.at[a])
        wait_for(dst, out_recv.at[a])


def local(queries, keys, values, out_grad, memory_frames, frame_tokens):
    groups = lax.axis_size("frame")
    zs = lax.axis_size("head")
    part, feat = queries.shape
    heads = feat // HEAD_DIM // zs
    slots = memory_frames.shape[1]
    mem_rows = slots * TF
    key_rows = -(-(ROWS + mem_rows) // 128) * 128
    g = lax.axis_index("frame")
    slot_ids = jnp.arange(slots, dtype=jnp.int32)

    mine = lax.dynamic_index_in_dim(memory_frames, g, 0, keepdims=False)
    all_frames = jnp.arange(frame_tokens.shape[0], dtype=jnp.int32)
    mem_counts = jnp.sum(
        jnp.where(mine[:, None] == all_frames[None, :], frame_tokens[None, :], 0), axis=1
    )
    own_counts = lax.dynamic_slice_in_dim(frame_tokens, g * FRAMES_DEV, FRAMES_DEV)
    counts = jnp.concatenate(
        [own_counts, mem_counts, jnp.zeros((key_rows // TF - FRAMES_DEV - slots,), jnp.int32)]
    )
    live = jnp.arange(TF, dtype=jnp.int32)[None, :] < counts[:, None]
    bias = jnp.where(live, 0.0, -jnp.inf).astype(jnp.float32).reshape(1, key_rows)

    askers = (g + 1 + slot_ids) % groups
    hit = jnp.arange(groups, dtype=jnp.int32)[:, None] == askers[None, :]
    wanted = jnp.sum(jnp.where(hit, memory_frames, 0), axis=0) % FRAMES_DEV
    mem_at = (wanted[:, None] * TF + jnp.arange(TF, dtype=jnp.int32)[None, :]).reshape(mem_rows)
    row_ids = jnp.arange(ROWS, dtype=jnp.int32)
    pick = (mem_at[:, None] == row_ids[None, :]).astype(jnp.bfloat16)
    spread = (row_ids[:, None] == mem_at[None, :]).astype(jnp.bfloat16)

    dims = (groups, zs, heads, slots, part, key_rows)
    any_spec = pl.BlockSpec(memory_space=pl.ANY)
    vmem_spec = pl.BlockSpec(memory_space=pltpu.VMEM)
    bf16 = jnp.bfloat16
    pairs = heads * ROWS * key_rows
    return pl.pallas_call(
        functools.partial(attention_kernel, dims),
        out_shape=[jax.ShapeDtypeStruct((part, feat), bf16)] * 4,
        in_specs=[any_spec] * 4 + [vmem_spec] * 3,
        out_specs=[any_spec] * 4,
        scratch_shapes=[
            pltpu.VMEM((heads, 2, ROWS, HEAD_DIM), bf16),
            pltpu.VMEM((heads, 2, key_rows, HEAD_DIM), bf16),
            pltpu.VMEM((heads, 2, mem_rows, HEAD_DIM), bf16),
            pltpu.VMEM((heads, 2, mem_rows, HEAD_DIM), bf16),
            pltpu.VMEM((heads, 2, mem_rows, HEAD_DIM), bf16),
            pltpu.VMEM((heads, 4, ROWS, HEAD_DIM), bf16),
            pltpu.VMEM((2, 2, key_rows, HEAD_DIM), jnp.float32),
            pltpu.SemaphoreType.DMA((4,)),
            pltpu.SemaphoreType.DMA((heads, 4)),
            pltpu.SemaphoreType.DMA,
            pltpu.SemaphoreType.DMA((heads,)),
            pltpu.SemaphoreType.DMA,
            pltpu.SemaphoreType.DMA((heads,)),
            pltpu.SemaphoreType.DMA((4,)),
            pltpu.SemaphoreType.DMA((4,)),
        ],
        compiler_params=pltpu.CompilerParams(
            collective_id=0, has_side_effects=True, vmem_limit_bytes=60 * 1024 * 1024
        ),
        cost_estimate=pl.CostEstimate(
            flops=10 * pairs * HEAD_DIM, bytes_accessed=16 * part * feat, transcendentals=pairs
        ),
    )(queries, keys, values, out_grad, bias, pick, spread)


def solution(mesh):
    rows = P(("frame", "head"), None)
    return jax.shard_map(
        local,
        mesh=mesh,
        in_specs=(rows, rows, rows, rows, P(), P()),
        out_specs=(rows, rows, rows, rows),
        check_vma=False,
    )
```

```python
import functools
import math

import jax
import jax.numpy as jnp
from jax import lax
from jax.experimental import pallas as pl
from jax.experimental.pallas import tpu as pltpu
from jax.sharding import PartitionSpec as P

HEAD_DIM = 128
TF = 64
FRAMES_DEV = 16
ROWS = FRAMES_DEV * TF
QBLOCK = 256
AHEAD = 4
MESH = pl.DeviceIdType.MESH


def attention_kernel(
    dims,
    q_in, k_in, v_in, g_in, frames_ref, tokens_ref,
    o_out, dq_out, dk_out, dv_out,
    bias_ref, pick_ref, spread_ref, qg, kv, mem_send, mem_grad, back, outs, acc,
    in_send, in_recv, mem_ssem, mem_rsem, back_ssem, back_rsem, out_send, out_recv,
):
    groups, zs, heads, slots, part, key_rows = dims
    mem_rows = slots * TF
    scale = 1.0 / math.sqrt(HEAD_DIM)
    g = lax.axis_index("frame")
    z = lax.axis_index("head")

    barrier = pltpu.get_barrier_semaphore()
    offsets = sorted({(1 + i) % groups for i in range(slots)} | {(-1 - i) % groups for i in range(slots)})
    for off in offsets:
        pl.semaphore_signal(
            barrier, inc=1, device_id={"frame": lax.rem(g + off, groups)}, device_id_type=MESH
        )
    for off in range(1, zs):
        pl.semaphore_signal(
            barrier, inc=1, device_id={"head": lax.rem(z + off, zs)}, device_id_type=MESH
        )
    pl.semaphore_wait(barrier, len(offsets) + zs - 1)

    my_rows = pl.ds(pl.multiple_of(z * part, part), part)

    def landing(h, a, rows):
        if a < 2:
            return kv.at[h, a, rows]
        return qg.at[h, a - 2, rows]

    def send_inputs(h):
        for a, src in enumerate((k_in, v_in, q_in, g_in)):
            for off in range(1, zs):
                peer = lax.rem(z + off, zs)
                cols = pl.ds(pl.multiple_of((peer * heads + h) * HEAD_DIM, HEAD_DIM), HEAD_DIM)
                pltpu.make_async_remote_copy(
                    src_ref=src.at[:, cols],
                    dst_ref=landing(h, a, my_rows),
                    send_sem=in_send.at[a],
                    recv_sem=in_recv.at[h, a],
                    device_id={"head": peer},
                    device_id_type=MESH,
                ).start()
            cols = pl.ds(pl.multiple_of((z * heads + h) * HEAD_DIM, HEAD_DIM), HEAD_DIM)
            pltpu.make_async_copy(
                src.at[:, cols], landing(h, a, my_rows), in_recv.at[h, a]
            ).start()

    def wait_for(ref, sem):
        pltpu.make_async_copy(ref, ref, sem).wait()

    def send_output(h, a):
        dst = (o_out, dq_out, dk_out, dv_out)[a]
        cols = pl.ds(pl.multiple_of((z * heads + h) * HEAD_DIM, HEAD_DIM), HEAD_DIM)
        for off in range(1, zs):
            peer = lax.rem(z + off, zs)
            pltpu.make_async_remote_copy(
                src_ref=outs.at[h, a, pl.ds(pl.multiple_of(peer * part, part), part)],
                dst_ref=dst.at[:, cols],
                send_sem=out_send.at[a],
                recv_sem=out_recv.at[a],
                device_id={"head": peer},
                device_id_type=MESH,
            ).start()
        pltpu.make_async_copy(outs.at[h, a, my_rows], dst.at[:, cols], out_recv.at[a]).start()

    lax.fori_loop(0, min(AHEAD, heads), lambda h, c: (send_inputs(h), c)[1], 0)

    wanted = [
        lax.rem(frames_ref[lax.rem(g + 1 + i, groups), i], FRAMES_DEV) * TF for i in range(slots)
    ]
    counts = [tokens_ref[g * FRAMES_DEV + f] for f in range(FRAMES_DEV)]
    counts += [tokens_ref[frames_ref[g, i]] for i in range(slots)]

    def chosen(shape, dim, entries):
        place = lax.broadcasted_iota(jnp.int32, shape, dim)
        segment = place // TF
        picked = jnp.zeros(shape, jnp.int32)
        for number, entry in enumerate(entries):
            picked = jnp.where(segment == number, entry, picked)
        return place - segment * TF, picked

    place, count = chosen((1, key_rows), 1, counts)
    bias_ref[...] = jnp.where(place < count, 0.0, -jnp.inf).astype(jnp.float32)
    place, start = chosen((mem_rows, 1), 0, wanted)
    columns = lax.broadcasted_iota(jnp.int32, (mem_rows, ROWS), 1)
    pick_ref[...] = jnp.where(columns == place + start, 1.0, 0.0).astype(jnp.bfloat16)
    place, start = chosen((1, mem_rows), 1, wanted)
    row_ids = lax.broadcasted_iota(jnp.int32, (ROWS, mem_rows), 0)
    spread_ref[...] = jnp.where(row_ids == place + start, 1.0, 0.0).astype(jnp.bfloat16)

    if key_rows > ROWS + mem_rows:
        rest = key_rows - ROWS - mem_rows

        def clear(h, c):
            kv[h, :, ROWS + mem_rows :, :] = jnp.zeros((2, rest, HEAD_DIM), jnp.bfloat16)
            return c

        lax.fori_loop(0, heads, clear, 0)

    def fetch(h):
        for a in range(2):
            wait_for(landing(h, a, pl.ds(0, ROWS)), in_recv.at[h, a])
        for a in range(2):
            mem_send[h, a] = jnp.dot(
                pick_ref[...], kv[h, a, :ROWS, :], preferred_element_type=jnp.float32
            ).astype(jnp.bfloat16)
        for i in range(slots):
            pltpu.make_async_remote_copy(
                src_ref=mem_send.at[h, :, pl.ds(i * TF, TF)],
                dst_ref=kv.at[h, :, pl.ds(ROWS + i * TF, TF)],
                send_sem=mem_ssem,
                recv_sem=mem_rsem.at[h],
                device_id={"frame": lax.rem(g + 1 + i, groups)},
                device_id_type=MESH,
            ).start()

    def attend(h):
        slot = lax.rem(h, 2)
        for a in range(2, 4):
            wait_for(landing(h, a, pl.ds(0, ROWS)), in_recv.at[h, a])
        wait_for(kv.at[h, :, pl.ds(ROWS, mem_rows)], mem_rsem.at[h])
        acc[slot] = jnp.zeros(acc.shape[1:], jnp.float32)

        def block(b, c):
            rows = pl.ds(pl.multiple_of(b * QBLOCK, QBLOCK), QBLOCK)
            query = qg[h, 0, rows, :]
            grad = qg[h, 1, rows, :]
            key = kv[h, 0]
            value = kv[h, 1]
            s = lax.dot_general(
                query, key, (((1,), (1,)), ((), ())), preferred_element_type=jnp.float32
            )
            s = s * (scale * math.log2(math.e)) + bias_ref[...]
            p = jnp.exp2(s - jnp.max(s, axis=1, keepdims=True))
            w = p * (1.0 / jnp.sum(p, axis=1, keepdims=True))
            wb = w.astype(jnp.bfloat16)
            outs[h, 0, rows, :] = jnp.dot(
                wb, value, preferred_element_type=jnp.float32
            ).astype(jnp.bfloat16)
            dp = lax.dot_general(
                grad, value, (((1,), (1,)), ((), ())), preferred_element_type=jnp.float32
            )
            delta = jnp.sum(w * dp, axis=1, keepdims=True)
            ds = (w * (dp - delta)).astype(jnp.bfloat16)
            outs[h, 1, rows, :] = (
                jnp.dot(ds, key, preferred_element_type=jnp.float32) * scale
            ).astype(jnp.bfloat16)
            acc[slot, 0] += lax.dot_general(
                ds, query, (((0,), (0,)), ((), ())), preferred_element_type=jnp.float32
            )
            acc[slot, 1] += lax.dot_general(
                wb, grad, (((0,), (0,)), ((), ())), preferred_element_type=jnp.float32
            )
            return c

        lax.fori_loop(0, ROWS // QBLOCK, block, 0)
        mem = pl.ds(ROWS, mem_rows)
        mem_grad[h, 0] = (acc[slot, 0, mem, :] * scale).astype(jnp.bfloat16)
        mem_grad[h, 1] = acc[slot, 1, mem, :].astype(jnp.bfloat16)
        for i in range(slots):
            pltpu.make_async_remote_copy(
                src_ref=mem_grad.at[h, :, pl.ds(i * TF, TF)],
                dst_ref=back.at[h, :, pl.ds(i * TF, TF)],
                send_sem=back_ssem,
                recv_sem=back_rsem.at[h],
                device_id={"frame": lax.rem(g + groups - 1 - i, groups)},
                device_id_type=MESH,
            ).start()
        send_output(h, 0)
        send_output(h, 1)

    def finish(h):
        slot = lax.rem(h, 2)
        wait_for(back.at[h], back_rsem.at[h])
        for a in range(2):
            extra = jnp.dot(spread_ref[...], back[h, a], preferred_element_type=jnp.float32)
            own = acc[slot, a, :ROWS, :]
            if a == 0:
                own = own * scale
            outs[h, 2 + a] = (own + extra).astype(jnp.bfloat16)
            send_output(h, 2 + a)

    def step(t, c):
        @pl.when(t < heads - AHEAD)
        def _():
            send_inputs(t + AHEAD)

        @pl.when(t < heads)
        def _():
            fetch(t)

        @pl.when(t >= 2)
        def _():
            finish(t - 2)

        @pl.when(jnp.logical_and(t >= 1, t <= heads))
        def _():
            attend(t - 1)

        return c

    lax.fori_loop(0, heads + 2, step, 0)

    sent = pl.ds(0, (zs - 1) * heads * HEAD_DIM)
    for a, src in enumerate((k_in, v_in, q_in, g_in)):
        wait_for(src.at[:, sent], in_send.at[a])
    wait_for(mem_send, mem_ssem)
    wait_for(mem_grad, back_ssem)
    for a, dst in enumerate((o_out, dq_out, dk_out, dv_out)):
        wait_for(outs.at[:, a, pl.ds(0, (zs - 1) * part)], out_send.at[a])
        wait_for(dst, out_recv.at[a])


def local(queries, keys, values, out_grad, memory_frames, frame_tokens):
    groups = lax.axis_size("frame")
    zs = lax.axis_size("head")
    part, feat = queries.shape
    heads = feat // HEAD_DIM // zs
    slots = memory_frames.shape[1]
    mem_rows = slots * TF
    key_rows = -(-(ROWS + mem_rows) // 128) * 128
    dims = (groups, zs, heads, slots, part, key_rows)
    any_spec = pl.BlockSpec(memory_space=pl.ANY)
    smem_spec = pl.BlockSpec(memory_space=pltpu.SMEM)
    bf16 = jnp.bfloat16
    pairs = heads * ROWS * key_rows
    return pl.pallas_call(
        functools.partial(attention_kernel, dims),
        out_shape=[jax.ShapeDtypeStruct((part, feat), bf16)] * 4,
        in_specs=[any_spec] * 4 + [smem_spec] * 2,
        out_specs=[any_spec] * 4,
        scratch_shapes=[
            pltpu.VMEM((1, key_rows), jnp.float32),
            pltpu.VMEM((mem_rows, ROWS), bf16),
            pltpu.VMEM((ROWS, mem_rows), bf16),
            pltpu.VMEM((heads, 2, ROWS, HEAD_DIM), bf16),
            pltpu.VMEM((heads, 2, key_rows, HEAD_DIM), bf16),
            pltpu.VMEM((heads, 2, mem_rows, HEAD_DIM), bf16),
            pltpu.VMEM((heads, 2, mem_rows, HEAD_DIM), bf16),
            pltpu.VMEM((heads, 2, mem_rows, HEAD_DIM), bf16),
            pltpu.VMEM((heads, 4, ROWS, HEAD_DIM), bf16),
            pltpu.VMEM((2, 2, key_rows, HEAD_DIM), jnp.float32),
            pltpu.SemaphoreType.DMA((4,)),
            pltpu.SemaphoreType.DMA((heads, 4)),
            pltpu.SemaphoreType.DMA,
            pltpu.SemaphoreType.DMA((heads,)),
            pltpu.SemaphoreType.DMA,
            pltpu.SemaphoreType.DMA((heads,)),
            pltpu.SemaphoreType.DMA((4,)),
            pltpu.SemaphoreType.DMA((4,)),
        ],
        compiler_params=pltpu.CompilerParams(
            collective_id=0, has_side_effects=True, vmem_limit_bytes=60 * 1024 * 1024
        ),
        cost_estimate=pl.CostEstimate(
            flops=10 * pairs * HEAD_DIM, bytes_accessed=16 * part * feat, transcendentals=pairs
        ),
    )(queries, keys, values, out_grad, memory_frames, frame_tokens)


def solution(mesh):
    rows = P(("frame", "head"), None)
    return jax.shard_map(
        local,
        mesh=mesh,
        in_specs=(rows, rows, rows, rows, P(), P()),
        out_specs=(rows, rows, rows, rows),
        check_vma=False,
    )
```
